32 devices in a mesh: parts: 2 (over y), blk: 16 (over z, x, core).
Axes of the slice: x: 2, y: 2, z: 4, core: 2. Of those that a mesh axis runs over, the one named last changes fastest.
Arguments:
- features: bfloat16 [8192, 128], P(('parts', 'blk')), parts along dimension 0, may hold values from -6 to 6
- w_first: bfloat16 [128, 256], replicated, may hold values from -0.5 to 0.5
- w_second: bfloat16 [256, 8192], replicated, may hold values from -0.375 to 0.375
- panel: bfloat16 [64, 64, 256], P(('parts', 'blk')), parts along dimension 0, may hold values from -6 to 6
- energies: float32 [256], replicated, may hold values from -1 to 1
- pair_dest: int32 [8192, 1], P(('parts', 'blk')), parts along dimension 0, may hold values from 0 to 15, as said below
- pair_row: int32 [8192], P(('parts', 'blk')), parts along dimension 0, may hold values from 0 to 1
- pair_col: int32 [8192], P(('parts', 'blk')), parts along dimension 0, may hold values from 0 to 1
Outputs:
- residual: float32 [64, 64, 256], P(('parts', 'blk')), parts along dimension 0
- loss: float32 [2], P('parts'), parts along dimension 0
- grad_first: float32 [256, 256], P('parts'), parts along dimension 0
- grad_second: float32 [512, 8192], P('parts', 'blk'), parts along dimension 0
The draws below stay inside these ranges and needn't reach their ends.
There are 2 independent parts, one for each index of `parts`. The reference program is written for one: setup_inputs(seed, part) draws one part's arguments, and reference() takes and returns one part's arrays. A program takes and returns all parts, laid end to end along the dimension named above; an argument that names none is the same for every part. Nothing has to cross between parts.
Inputs may be any that keep to these rules, and one draw needn't show every extreme that they name: `pair_dest`: among one device's 256 pairs at most 24 have their block row on one device; every device owns the block rows of exactly 24 of its own pairs. Owners lie mostly near the listing device along the axis.
All inputs are finite; a program needn't handle non-finite values.
Results may differ from the reference program's by a relative error of at most 0.004.
Values may be sent and summed in bfloat16 or wider, within the bound.
A program may use at most 128 MiB of HBM per device.

```python
import jax
import jax.numpy as jnp
from jax import lax

O = 64
P_SIZE = 256
F = 128
HID = 256
BLK_DEV = 2
PAIR_DEV = 256
NB = 32
PAIRS = 4096
N_BLK = 16


def draw_pair_dest(key, part):
    count_dev = N_BLK
    per_owner = 3 * PAIR_DEV // (2 * N_BLK)
    offsets = jnp.arange(count_dev, dtype=jnp.int32) - count_dev // 4
    spread = jnp.abs(offsets)
    slot_offset = jnp.repeat(offsets, per_owner, total_repeat_length=count_dev * per_owner)
    slot_spread = jnp.repeat(spread, per_owner, total_repeat_length=count_dev * per_owner)
    slot_total = count_dev * per_owner
    base_key = jax.random.fold_in(key, 7)

    def one_device(device):
        dev_key = jax.random.fold_in(base_key, device)
        first_key, second_key = jax.random.split(dev_key)
        raw = jax.random.randint(first_key, (slot_total,), 0, 4096, dtype=jnp.int32)
        base = jnp.where(slot_spread == 0, jnp.int32(8192), raw // (1 + slot_spread))
        score = base * slot_total + jnp.arange(slot_total, dtype=jnp.int32)
        unused_top, picked = lax.top_k(score, PAIR_DEV)
        chosen = slot_offset[picked]
        chosen = jax.random.permutation(second_key, chosen)
        return jnp.mod(device + chosen, count_dev).astype(jnp.int32)
    owners = jax.vmap(one_device)(jnp.arange(count_dev, dtype=jnp.int32))
    return owners.reshape(count_dev * PAIR_DEV, 1).astype(jnp.int32)


def place_ends(entries, rng, low, top_value):
    extent = entries.shape
    place = [jax.random.randint(jax.random.fold_in(rng, axis), (), 0, extent[axis]) for axis in range(len(extent))]
    entries = entries.at[tuple(place)].set(low)
    longest = extent.index(max(extent))
    place[longest] = (place[longest] + 1) % extent[longest]
    return entries.at[tuple(place)].set(top_value)


def block_scale(rng, shape, shards, smallest, top_value):
    def one(dim, blocks):
        steps = jax.random.uniform(jax.random.fold_in(jax.random.fold_in(rng, 6), dim), (blocks,), jnp.float32, smallest / len(shards), top_value / len(shards))
        return jnp.repeat(jnp.exp(steps), shape[dim] // blocks).reshape((-1,) + (1,) * (len(shape) - dim - 1))

    level = one(*shards[0])
    for cut in shards[1:]:
        level = level * one(*cut)
    return level


def normal_values(stream_key, extent, deviation, limit, cuts=(), kind=jnp.bfloat16):
    result = deviation * jax.random.normal(stream_key, extent, jnp.float32)
    if cuts:
        result = result * block_scale(stream_key, extent, cuts, -0.22, 0.18)
    return jnp.clip(result, -limit, limit).astype(kind)


def setup_inputs(seed: int = 0, part: int = 0) -> dict:
    seeds = jax.random.split(jax.random.key(seed), 9)
    part_splits = jax.random.split(jax.random.fold_in(seeds[8], part), 9)
    features = normal_values(part_splits[0], (PAIRS, F), 1.0, 6.0, ((0, 16),))
    w_first = normal_values(seeds[1], (F, HID), F ** -0.5, 0.5)
    w_second = normal_values(seeds[2], (HID, 2 * O * O), HID ** -0.5, 0.375)
    panel = normal_values(part_splits[3], (NB, O, P_SIZE), 1.0, 6.0, ((0, 16),))
    energies = jnp.clip(jax.random.uniform(seeds[4], (P_SIZE,), jnp.float32, -1.0, 1.0), -1.0, 1.0)
    pair_dest = draw_pair_dest(jax.random.fold_in(jax.random.fold_in(seeds[8], part), 71), part)
    pair_row = place_ends(jax.random.randint(part_splits[6], (PAIRS,), 0, BLK_DEV), jax.random.fold_in(part_splits[6], 1), 0, BLK_DEV - 1).astype(jnp.int32)
    pair_col = place_ends(jax.random.randint(part_splits[7], (PAIRS,), 0, BLK_DEV), jax.random.fold_in(part_splits[7], 1), 0, BLK_DEV - 1).astype(jnp.int32)
    return {"features": features, "w_first": w_first, "w_second": w_second, "panel": panel, "energies": energies, "pair_dest": pair_dest, "pair_row": pair_row, "pair_col": pair_col}


def predict(feats, w_first, w_second):
    pre = jnp.dot(feats, w_first, preferred_element_type=jnp.float32)
    hidden = jax.nn.silu(pre).astype(jnp.bfloat16)
    blocks = (jnp.dot(hidden, w_second, preferred_element_type=jnp.float32) / O).astype(jnp.bfloat16)
    return pre, hidden, blocks


def reference(features, w_first, w_second, panel, energies, pair_dest, pair_row, pair_col):
    total_blocks = BLK_DEV * N_BLK
    devices = jnp.arange(N_BLK, dtype=jnp.int32)
    feats_dev = features.reshape(N_BLK, PAIR_DEV, F)
    dest_dev = pair_dest[:, 0].reshape(N_BLK, PAIR_DEV).astype(jnp.int32)
    row_dev = pair_row.reshape(N_BLK, PAIR_DEV).astype(jnp.int32)
    col_dev = pair_col.reshape(N_BLK, PAIR_DEV).astype(jnp.int32)
    items = (devices, feats_dev, dest_dev, row_dev, col_dev)

    def forward(total, item):
        device, feats, dest, prow, pcol = item
        row_glob = (dest * BLK_DEV + prow).astype(jnp.int32)
        col_glob = (device * BLK_DEV + pcol).astype(jnp.int32)
        unused_pre, unused_hidden, blocks = predict(feats, w_first, w_second)
        blocks = blocks.reshape(PAIR_DEV, 2, O, O).astype(jnp.float32)
        coeffs = panel[col_glob].astype(jnp.float32)
        h_panel = jnp.einsum('sab,sbp->sap', blocks[:, 0], coeffs, precision=lax.Precision.HIGHEST)
        s_panel = jnp.einsum('sab,sbp->sap', blocks[:, 1], coeffs, precision=lax.Precision.HIGHEST)
        contrib = h_panel - s_panel * energies
        return total.at[row_glob].add(contrib), None

    residual = lax.scan(forward, jnp.zeros((total_blocks, O, P_SIZE), jnp.float32), items)[0]
    loss = (jnp.sum(residual * residual) / (total_blocks * O * P_SIZE)).reshape(1)
    grad_h = (residual / total_blocks).astype(jnp.bfloat16)
    grad_s = (-(residual * energies) / total_blocks).astype(jnp.bfloat16)

    def backward(carry, item):
        acc_first, acc_second = carry
        device, feats, dest, prow, pcol = item
        row_glob = (dest * BLK_DEV + prow).astype(jnp.int32)
        col_glob = (device * BLK_DEV + pcol).astype(jnp.int32)
        pre, hidden, unused_blocks = predict(feats, w_first, w_second)
        coeffs = panel[col_glob].astype(jnp.float32)
        gh_rows = grad_h[row_glob].astype(jnp.float32)
        gs_rows = grad_s[row_glob].astype(jnp.float32)
        d_h = jnp.einsum('sap,sbp->sab', gh_rows, coeffs, precision=lax.Precision.HIGHEST).astype(jnp.bfloat16)
        d_s = jnp.einsum('sap,sbp->sab', gs_rows, coeffs, precision=lax.Precision.HIGHEST).astype(jnp.bfloat16)
        d_flat = jnp.stack([d_h, d_s], axis=1).reshape(PAIR_DEV, 2 * O * O)
        acc_second = acc_second + jnp.dot(hidden.T, d_flat, preferred_element_type=jnp.float32) / O
        d_hidden = jnp.dot(d_flat, w_second.T, preferred_element_type=jnp.float32) / O
        sig = jax.nn.sigmoid(pre)
        d_pre = (d_hidden * sig * (1.0 + pre * (1.0 - sig))).astype(jnp.bfloat16)
        acc_first = acc_first + jnp.dot(feats.T, d_pre, preferred_element_type=jnp.float32)
        return (acc_first, acc_second), None

    start = (jnp.zeros((F, HID), jnp.float32), jnp.zeros((HID, 2 * O * O), jnp.float32))
    grad_first, grad_second = lax.scan(backward, start, items)[0]
    return (residual, loss, grad_first, grad_second)
```

```python
import jax
import jax.numpy as jnp
from jax import lax
from jax.sharding import PartitionSpec as P


def predict(feats, w_first, w_second, orbitals):
    pre = jnp.dot(feats, w_first, preferred_element_type=jnp.float32)
    hidden = jax.nn.silu(pre).astype(jnp.bfloat16)
    blocks = (jnp.dot(hidden, w_second, preferred_element_type=jnp.float32) / orbitals).astype(
        jnp.bfloat16
    )
    return (pre, hidden, blocks)


def weight_terms(feats, pre, hidden, d_flat, w_second, orbitals):
    term_second = jnp.dot(hidden.T, d_flat, preferred_element_type=jnp.float32) / orbitals
    d_hidden = (
        lax.dot_general(
            d_flat, w_second, (((1,), (1,)), ((), ())), preferred_element_type=jnp.float32
        )
        / orbitals
    )
    sig = jax.nn.sigmoid(pre)
    d_pre = (d_hidden * sig * (1.0 + pre * (1.0 - sig))).astype(jnp.bfloat16)
    term_first = jnp.dot(feats.T, d_pre, preferred_element_type=jnp.float32)
    return (term_first, term_second)


def slot_work(slot_blocks, slot_panel, slot_rows, energies, blk_dev, total_blocks):
    slots, unused_two, orbitals, unused_o = slot_blocks.shape
    columns = slot_panel.shape[2]
    group = 32
    steps_count = slots // group
    grouped = (
        slot_blocks.reshape(steps_count, group, 2, orbitals, orbitals),
        slot_panel.reshape(steps_count, group, orbitals, columns),
        slot_rows.reshape(steps_count, group),
    )
    row_ids = jnp.arange(blk_dev, dtype=jnp.int32)

    def forward(total, item):
        blocks, coeffs, rows = item
        h_panel = jnp.einsum(
            "sab,sbp->sap", blocks[:, 0], coeffs, preferred_element_type=jnp.float32
        )
        s_panel = jnp.einsum(
            "sab,sbp->sap", blocks[:, 1], coeffs, preferred_element_type=jnp.float32
        )
        contrib = h_panel - s_panel * energies
        selector = (rows[None, :] == row_ids[:, None]).astype(jnp.float32)
        added = jnp.einsum("rs,sap->rap", selector, contrib, precision=lax.Precision.HIGHEST)
        return (total + added, None)

    residual = lax.scan(forward, jnp.zeros((blk_dev, orbitals, columns), jnp.float32), grouped)[0]
    grad_h = (residual / total_blocks).astype(jnp.bfloat16)
    grad_s = (-(residual * energies) / total_blocks).astype(jnp.bfloat16)

    def backward(carry, item):
        blocks, coeffs, rows = item
        valid = (rows >= 0)[:, None, None]
        safe_rows = jnp.maximum(rows, 0)
        gh_rows = jnp.where(valid, grad_h[safe_rows], jnp.zeros((), jnp.bfloat16))
        gs_rows = jnp.where(valid, grad_s[safe_rows], jnp.zeros((), jnp.bfloat16))
        d_h = jnp.einsum(
            "sap,sbp->sab", gh_rows, coeffs, preferred_element_type=jnp.float32
        ).astype(jnp.bfloat16)
        d_s = jnp.einsum(
            "sap,sbp->sab", gs_rows, coeffs, preferred_element_type=jnp.float32
        ).astype(jnp.bfloat16)
        return (carry, jnp.stack([d_h, d_s], axis=1))

    d_blocks = lax.scan(backward, 0, grouped)[1]
    return (residual, d_blocks.reshape(slots, 2, orbitals, orbitals))


def local(features, w_first, w_second, panel, energies, pair_dest, pair_row, pair_col):
    n_dev = lax.axis_size("blk")
    my_index = lax.axis_index("blk")
    pair_count, feat_width = features.shape
    blk_dev, orbitals, columns = panel.shape
    capacity = 3 * pair_count // (2 * n_dev)
    slots = n_dev * capacity
    total_blocks = blk_dev * n_dev
    dest = pair_dest[:, 0]
    dest_table = (dest[:, None] == jnp.arange(n_dev, dtype=jnp.int32)[None, :]).astype(jnp.int32)
    rank_in = jnp.sum(jnp.cumsum(dest_table, axis=0) * dest_table, axis=1) - 1
    slot_of = dest * capacity + rank_in
    source = (
        jnp.full((slots,), pair_count, jnp.int32)
        .at[slot_of]
        .set(jnp.arange(pair_count, dtype=jnp.int32))
    )
    empty_label = jnp.full((1,), -1, jnp.int32)
    rows_sent = jnp.concatenate([pair_row, empty_label])[source]
    cols_sent = jnp.concatenate([my_index * blk_dev + pair_col, jnp.zeros((1,), jnp.int32)])[source]
    labels = jnp.stack([rows_sent, cols_sent], axis=-1).reshape(n_dev, capacity, 2)
    whole_panel = lax.all_gather(panel, "blk", axis=0, tiled=True)
    pre, hidden, blocks = predict(features, w_first, w_second, orbitals)
    padded = jnp.concatenate([blocks, jnp.zeros((1, blocks.shape[1]), jnp.bfloat16)], axis=0)
    send_blocks = padded[source].reshape(n_dev, capacity, 2, orbitals, orbitals)
    got_blocks, got_labels = (
        lax.all_to_all(send_blocks, "blk", split_axis=0, concat_axis=0, tiled=True),
        lax.all_to_all(labels, "blk", split_axis=0, concat_axis=0, tiled=True),
    )
    got_labels = got_labels.reshape(slots, 2)
    slot_panel = whole_panel[got_labels[:, 1]]
    residual, d_blocks = slot_work(
        got_blocks.reshape(slots, 2, orbitals, orbitals),
        slot_panel,
        got_labels[:, 0],
        energies,
        blk_dev,
        total_blocks,
    )
    back = lax.all_to_all(
        d_blocks.reshape(n_dev, capacity, 2, orbitals, orbitals),
        "blk",
        split_axis=0,
        concat_axis=0,
        tiled=True,
    )
    d_flat = back.reshape(slots, 2 * orbitals * orbitals)[slot_of]
    term_first, term_second = weight_terms(features, pre, hidden, d_flat, w_second, orbitals)
    grad_second = lax.psum_scatter(term_second, "blk", scatter_dimension=1, tiled=True)
    grad_first, square_sum = lax.psum((term_first, jnp.sum(residual * residual)), "blk")
    loss = (square_sum / (total_blocks * orbitals * columns)).reshape(1)
    return (residual, loss, grad_first, grad_second)


def fast_local(features, w_first, w_second, panel, energies, pair_dest, pair_row, pair_col):
    n_dev = lax.axis_size("blk")
    me = lax.axis_index("blk")
    pairs, width = features.shape
    blk_dev, orbitals, columns = panel.shape
    hid = w_second.shape[0]
    blocks = blk_dev * n_dev
    groups = blk_dev * blocks
    half = n_dev // 2
    a_count = orbitals // half
    side = me // half
    spot = me % half
    f32 = jnp.float32
    gid = pair_col * blocks + pair_dest[:, 0] * blk_dev + pair_row
    feats = lax.all_gather(features, "blk", axis=0, tiled=True)
    gids = lax.all_gather(gid, "blk", axis=0, tiled=False)
    coeffs = lax.all_gather(panel, "blk", axis=0, tiled=True)
    pre = jnp.dot(feats, w_first, preferred_element_type=f32)
    sig = jax.nn.sigmoid(pre)
    hidden = (pre * sig).astype(jnp.bfloat16)
    onehot = (gids[:, None, :] == jnp.arange(groups, dtype=jnp.int32)[None, :, None]).astype(jnp.bfloat16)
    summed = jnp.einsum("dgp,dpk->dgk", onehot, hidden.reshape(n_dev, pairs, hid), preferred_element_type=f32)
    summed = summed.astype(jnp.bfloat16).reshape(n_dev * groups, hid)
    w_sides = w_second.reshape(hid, 2, orbitals * orbitals)
    w_part = lax.dynamic_slice_in_dim(w_sides, spot * a_count * orbitals, a_count * orbitals, 2)
    w_own = lax.dynamic_index_in_dim(w_part, side, 1, keepdims=False)
    mats = jnp.dot(summed, w_part.reshape(hid, -1), preferred_element_type=f32) / orbitals
    mats = mats.astype(jnp.bfloat16).reshape(blocks, blocks, 2, a_count, orbitals)
    both = jnp.einsum("crhab,cbp->hrap", mats, coeffs, preferred_element_type=f32)
    resid = both[0] - both[1] * energies
    grad = jnp.where(side == 0, resid / blocks, -(resid * energies) / blocks).astype(jnp.bfloat16)
    d_mats = jnp.einsum("rap,cbp->crab", grad, coeffs, preferred_element_type=f32)
    d_mats = d_mats.astype(jnp.bfloat16).reshape(blocks * blocks, a_count * orbitals)
    grad_second = jnp.dot(summed.T, d_mats, preferred_element_type=f32) / orbitals
    d_sum = lax.dot_general(d_mats, w_own, (((1,), (1,)), ((), ())), preferred_element_type=f32) / orbitals
    d_sum = d_sum.astype(jnp.bfloat16).reshape(n_dev, groups, hid)
    d_hidden = jnp.einsum("dgp,dgk->dpk", onehot, d_sum, preferred_element_type=f32).reshape(-1, hid)
    d_pre = (d_hidden * sig * (1.0 + pre * (1.0 - sig))).astype(jnp.bfloat16)
    term_first = jnp.dot(feats.T, d_pre, preferred_element_type=f32)
    mine = lax.dynamic_slice_in_dim(resid, side * (blocks // 2), blocks // 2, 0)
    mine = mine.reshape(half, blk_dev, a_count, columns)
    sides = [list(range(half)), list(range(half, n_dev))]
    got = lax.all_to_all(mine, "blk", 0, 0, axis_index_groups=sides, tiled=True)
    residual = got.transpose(1, 0, 2, 3).reshape(blk_dev, orbitals, columns)
    grad_first, square_sum = lax.psum((term_first, 0.5 * jnp.sum(resid * resid)), "blk")
    loss = (square_sum / (blocks * orbitals * columns)).reshape(1)
    return (residual, loss, grad_first, grad_second)


def solution(mesh):
    in_specs = (
        P(("parts", "blk"), None),
        P(),
        P(),
        P(("parts", "blk"), None, None),
        P(),
        P(("parts", "blk"), None),
        P(("parts", "blk")),
        P(("parts", "blk")),
    )
    out_specs = (P(("parts", "blk"), None, None), P("parts"), P("parts", None), P("parts", "blk"))
    return jax.shard_map(
        fast_local if mesh.shape["blk"] <= 32 else local, mesh=mesh, in_specs=in_specs, out_specs=out_specs, check_vma=False)
```

```python
import jax
import jax.numpy as jnp
from jax import lax
from jax.experimental import pallas as pl
from jax.experimental.pallas import tpu as pltpu
from jax.sharding import PartitionSpec as P


def predict(feats, w_first, w_second, orbitals):
    pre = jnp.dot(feats, w_first, preferred_element_type=jnp.float32)
    hidden = jax.nn.silu(pre).astype(jnp.bfloat16)
    blocks = (jnp.dot(hidden, w_second, preferred_element_type=jnp.float32) / orbitals).astype(
        jnp.bfloat16
    )
    return (pre, hidden, blocks)


def weight_terms(feats, pre, hidden, d_flat, w_second, orbitals):
    term_second = jnp.dot(hidden.T, d_flat, preferred_element_type=jnp.float32) / orbitals
    d_hidden = (
        lax.dot_general(
            d_flat, w_second, (((1,), (1,)), ((), ())), preferred_element_type=jnp.float32
        )
        / orbitals
    )
    sig = jax.nn.sigmoid(pre)
    d_pre = (d_hidden * sig * (1.0 + pre * (1.0 - sig))).astype(jnp.bfloat16)
    term_first = jnp.dot(feats.T, d_pre, preferred_element_type=jnp.float32)
    return (term_first, term_second)


def slot_work(slot_blocks, slot_panel, slot_rows, energies, blk_dev, total_blocks):
    slots, unused_two, orbitals, unused_o = slot_blocks.shape
    columns = slot_panel.shape[2]
    group = 32
    steps_count = slots // group
    grouped = (
        slot_blocks.reshape(steps_count, group, 2, orbitals, orbitals),
        slot_panel.reshape(steps_count, group, orbitals, columns),
        slot_rows.reshape(steps_count, group),
    )
    row_ids = jnp.arange(blk_dev, dtype=jnp.int32)

    def forward(total, item):
        blocks, coeffs, rows = item
        h_panel = jnp.einsum(
            "sab,sbp->sap", blocks[:, 0], coeffs, preferred_element_type=jnp.float32
        )
        s_panel = jnp.einsum(
            "sab,sbp->sap", blocks[:, 1], coeffs, preferred_element_type=jnp.float32
        )
        contrib = h_panel - s_panel * energies
        selector = (rows[None, :] == row_ids[:, None]).astype(jnp.float32)
        added = jnp.einsum("rs,sap->rap", selector, contrib, precision=lax.Precision.HIGHEST)
        return (total + added, None)

    residual = lax.scan(forward, jnp.zeros((blk_dev, orbitals, columns), jnp.float32), grouped)[0]
    grad_h = (residual / total_blocks).astype(jnp.bfloat16)
    grad_s = (-(residual * energies) / total_blocks).astype(jnp.bfloat16)

    def backward(carry, item):
        blocks, coeffs, rows = item
        valid = (rows >= 0)[:, None, None]
        safe_rows = jnp.maximum(rows, 0)
        gh_rows = jnp.where(valid, grad_h[safe_rows], jnp.zeros((), jnp.bfloat16))
        gs_rows = jnp.where(valid, grad_s[safe_rows], jnp.zeros((), jnp.bfloat16))
        d_h = jnp.einsum(
            "sap,sbp->sab", gh_rows, coeffs, preferred_element_type=jnp.float32
        ).astype(jnp.bfloat16)
        d_s = jnp.einsum(
            "sap,sbp->sab", gs_rows, coeffs, preferred_element_type=jnp.float32
        ).astype(jnp.bfloat16)
        return (carry, jnp.stack([d_h, d_s], axis=1))

    d_blocks = lax.scan(backward, 0, grouped)[1]
    return (residual, d_blocks.reshape(slots, 2, orbitals, orbitals))


def local(features, w_first, w_second, panel, energies, pair_dest, pair_row, pair_col):
    n_dev = lax.axis_size("blk")
    my_index = lax.axis_index("blk")
    pair_count, feat_width = features.shape
    blk_dev, orbitals, columns = panel.shape
    capacity = 3 * pair_count // (2 * n_dev)
    slots = n_dev * capacity
    total_blocks = blk_dev * n_dev
    dest = pair_dest[:, 0]
    dest_table = (dest[:, None] == jnp.arange(n_dev, dtype=jnp.int32)[None, :]).astype(jnp.int32)
    rank_in = jnp.sum(jnp.cumsum(dest_table, axis=0) * dest_table, axis=1) - 1
    slot_of = dest * capacity + rank_in
    source = (
        jnp.full((slots,), pair_count, jnp.int32)
        .at[slot_of]
        .set(jnp.arange(pair_count, dtype=jnp.int32))
    )
    empty_label = jnp.full((1,), -1, jnp.int32)
    rows_sent = jnp.concatenate([pair_row, empty_label])[source]
    cols_sent = jnp.concatenate([my_index * blk_dev + pair_col, jnp.zeros((1,), jnp.int32)])[source]
    labels = jnp.stack([rows_sent, cols_sent], axis=-1).reshape(n_dev, capacity, 2)
    whole_panel = lax.all_gather(panel, "blk", axis=0, tiled=True)
    pre, hidden, blocks = predict(features, w_first, w_second, orbitals)
    padded = jnp.concatenate([blocks, jnp.zeros((1, blocks.shape[1]), jnp.bfloat16)], axis=0)
    send_blocks = padded[source].reshape(n_dev, capacity, 2, orbitals, orbitals)
    got_blocks, got_labels = (
        lax.all_to_all(send_blocks, "blk", split_axis=0, concat_axis=0, tiled=True),
        lax.all_to_all(labels, "blk", split_axis=0, concat_axis=0, tiled=True),
    )
    got_labels = got_labels.reshape(slots, 2)
    slot_panel = whole_panel[got_labels[:, 1]]
    residual, d_blocks = slot_work(
        got_blocks.reshape(slots, 2, orbitals, orbitals),
        slot_panel,
        got_labels[:, 0],
        energies,
        blk_dev,
        total_blocks,
    )
    back = lax.all_to_all(
        d_blocks.reshape(n_dev, capacity, 2, orbitals, orbitals),
        "blk",
        split_axis=0,
        concat_axis=0,
        tiled=True,
    )
    d_flat = back.reshape(slots, 2 * orbitals * orbitals)[slot_of]
    term_first, term_second = weight_terms(features, pre, hidden, d_flat, w_second, orbitals)
    grad_second = lax.psum_scatter(term_second, "blk", scatter_dimension=1, tiled=True)
    grad_first, square_sum = lax.psum((term_first, jnp.sum(residual * residual)), "blk")
    loss = (square_sum / (total_blocks * orbitals * columns)).reshape(1)
    return (residual, loss, grad_first, grad_second)


VMEM = pl.BlockSpec(memory_space=pltpu.VMEM)
MESH = pl.DeviceIdType.MESH


def greet(partners):
    barrier = pltpu.get_barrier_semaphore()
    for other in partners:
        pl.semaphore_signal(barrier, inc=1, device_id={"blk": other}, device_id_type=MESH)
    pl.semaphore_wait(barrier, len(partners))


def gather_kernel(n, count, *refs):
    ins, outs = refs[:count], refs[count : 2 * count]
    send_sem, recv_sem, local_sem = refs[2 * count :]
    me = lax.axis_index("blk")
    depth = n // 4
    z, x, core = me // 4, (me // 2) % 2, me % 2

    def at(zz, xx, cc):
        return zz * 4 + xx * 2 + cc

    x_peer, core_peer = at(z, 1 - x, core), at(z, x, 1 - core)
    z_peers = [at((z + d) % depth, x, core) for d in range(1, depth)]
    greet([x_peer, core_peer] + z_peers)

    def copy(arr, source, block, peer, kind):
        return pltpu.make_async_remote_copy(
            src_ref=source,
            dst_ref=outs[arr].at[block],
            send_sem=send_sem.at[arr, block, kind],
            recv_sem=recv_sem.at[arr, block],
            device_id={"blk": peer},
            device_id_type=MESH,
        )

    started = []

    def send(arr, block, peer, kind, source=None):
        item = copy(arr, outs[arr].at[block] if source is None else source, block, peer, kind)
        item.start()
        started.append(item)

    def arrived(arr, block):
        copy(arr, outs[arr].at[block], block, core_peer, 0).wait_recv()

    own = []
    for arr in range(count):
        for k, peer in enumerate(z_peers):
            send(arr, me, peer, 2 + k, ins[arr])
        send(arr, me, x_peer, 0, ins[arr])
        send(arr, me, core_peer, 1, ins[arr])
        item = pltpu.make_async_copy(ins[arr], outs[arr].at[me], local_sem.at[arr])
        item.start()
        own.append(item)
    for arr in range(count):
        arrived(arr, x_peer)
        send(arr, x_peer, core_peer, 1)
        for block in z_peers:
            arrived(arr, block)
            send(arr, block, x_peer, 0)
            send(arr, block, core_peer, 1)
    for arr in range(count):
        for d in range(1, depth):
            block = at((z + d) % depth, 1 - x, core)
            arrived(arr, block)
            send(arr, block, core_peer, 1)
    for arr in range(count):
        for d in range(depth):
            for xx in range(2):
                arrived(arr, at((z + d) % depth, xx, 1 - core))
        own[arr].wait()
    for item in started:
        item.wait_send()


def gather_all(n, arrays):
    count = len(arrays)
    return pl.pallas_call(
        lambda *refs: gather_kernel(n, count, *refs),
        out_shape=[jax.ShapeDtypeStruct((n,) + a.shape, a.dtype) for a in arrays],
        in_specs=[VMEM] * count,
        out_specs=[VMEM] * count,
        scratch_shapes=[
            pltpu.SemaphoreType.DMA((count, n, 1 + n // 4)),
            pltpu.SemaphoreType.DMA((count, n)),
            pltpu.SemaphoreType.DMA((count,)),
        ],
        compiler_params=pltpu.CompilerParams(
            collective_id=0, has_side_effects=True, vmem_limit_bytes=32 * 2**20
        ),
        name="gather_all",
    )(*arrays)


def finish_kernel(n, term, square, mine, first, loss, resid, land, loss_land, total, *sems):
    send_t, recv_t, send_l, recv_l, send_r, recv_r, send_g, recv_g = sems
    me = lax.axis_index("blk")
    half = n // 2
    side, spot = me // half, me % half
    rows = mine.shape[2]
    others = [(me + k) % n for k in range(1, n)]
    greet(others)

    def copy(src, dst, send_sem, recv_sem, peer):
        return pltpu.make_async_remote_copy(
            src_ref=src,
            dst_ref=dst,
            send_sem=send_sem,
            recv_sem=recv_sem,
            device_id={"blk": peer},
            device_id_type=MESH,
        )

    started = []
    for k, peer in enumerate(others):
        started.append(copy(term.at[peer], land.at[me], send_t.at[k], recv_t.at[me], peer))
        started.append(copy(square, loss_land.at[me], send_l.at[k], recv_l.at[me], peer))
    for k in range(1, half):
        near = (spot + k) % half
        started.append(
            copy(
                mine.at[near],
                resid.at[:, pl.ds(pl.multiple_of(spot * rows, 8), rows), :],
                send_r.at[k],
                recv_r.at[spot],
                side * half + near,
            )
        )
    for item in started:
        item.start()
    land[me] = term[me]
    loss_land[me] = square[...]
    resid[:, pl.ds(pl.multiple_of(spot * rows, 8), rows), :] = mine[spot]
    for peer in others:
        copy(term.at[me], land.at[peer], send_t.at[0], recv_t.at[peer], peer).wait_recv()
    added = land[0]
    for d in range(1, n):
        added = added + land[d]
    total[...] = added
    final = []
    for k, peer in enumerate(others):
        item = copy(total, first.at[me], send_g.at[k], recv_g.at[me], peer)
        item.start()
        final.append(item)
    first[me] = added
    for peer in others:
        copy(square, loss_land.at[peer], send_l.at[0], recv_l.at[peer], peer).wait_recv()
    squares = loss_land[0]
    for d in range(1, n):
        squares = squares + loss_land[d]
    loss[...] = squares
    for k in range(1, half):
        near = (spot + k) % half
        copy(
            mine.at[near],
            resid.at[:, pl.ds(pl.multiple_of(near * rows, 8), rows), :],
            send_r.at[k],
            recv_r.at[near],
            side * half + near,
        ).wait_recv()
    for peer in others:
        copy(total, first.at[peer], send_g.at[0], recv_g.at[peer], peer).wait_recv()
    for item in started + final:
        item.wait_send()


def finish(n, term, square, mine):
    half, blk_dev, rows, columns = mine.shape
    dma = pltpu.SemaphoreType.DMA
    return pl.pallas_call(
        lambda *refs: finish_kernel(n, *refs),
        out_shape=[
            jax.ShapeDtypeStruct(term.shape, jnp.float32),
            jax.ShapeDtypeStruct(square.shape, jnp.float32),
            jax.ShapeDtypeStruct((blk_dev, half * rows, columns), jnp.float32),
        ],
        in_specs=[VMEM] * 3,
        out_specs=[VMEM] * 3,
        scratch_shapes=[
            pltpu.VMEM(term.shape, jnp.float32),
            pltpu.VMEM((n,) + square.shape, jnp.float32),
            pltpu.VMEM(term.shape[1:], jnp.float32),
        ]
        + [dma((n,))] * 8,
        compiler_params=pltpu.CompilerParams(
            collective_id=1, has_side_effects=True, vmem_limit_bytes=32 * 2**20
        ),
        name="finish",
    )(term, square, mine)


def fast_local(features, w_first, w_second, panel, energies, pair_dest, pair_row, pair_col):
    n_dev = lax.axis_size("blk")
    me = lax.axis_index("blk")
    pairs, width = features.shape
    blk_dev, orbitals, columns = panel.shape
    hid = w_second.shape[0]
    blocks = blk_dev * n_dev
    groups = blk_dev * blocks
    half = n_dev // 2
    a_count = orbitals // half
    side = me // half
    spot = me % half
    f32 = jnp.float32
    gid = pair_col * blocks + pair_dest[:, 0] * blk_dev + pair_row
    ids = jnp.broadcast_to(gid.reshape(1, pairs), (8, pairs))
    feats, gids, coeffs = gather_all(
        n_dev, (features, ids, panel.reshape(blk_dev * orbitals, columns))
    )
    feats = feats.reshape(n_dev * pairs, width)
    gids = gids[:, 0, :]
    coeffs = coeffs.reshape(blocks, orbitals, columns)
    pre = jnp.dot(feats, w_first, preferred_element_type=f32)
    sig = jax.nn.sigmoid(pre)
    hidden = (pre * sig).astype(jnp.bfloat16)
    onehot = (gids[:, None, :] == jnp.arange(groups, dtype=jnp.int32)[None, :, None]).astype(jnp.bfloat16)
    summed = jnp.einsum("dgp,dpk->dgk", onehot, hidden.reshape(n_dev, pairs, hid), preferred_element_type=f32)
    summed = summed.astype(jnp.bfloat16).reshape(n_dev * groups, hid)
    span = a_count * orbitals
    w_part = jnp.concatenate(
        [
            lax.dynamic_slice_in_dim(w_second, part * orbitals * orbitals + spot * span, span, 1)
            for part in range(2)
        ],
        axis=1,
    )
    w_own = lax.dynamic_slice_in_dim(w_second, me * span, span, 1)
    mats = jnp.dot(summed, w_part, preferred_element_type=f32) / orbitals
    mats = mats.astype(jnp.bfloat16).reshape(blocks, blocks, 2, a_count, orbitals)
    both = jnp.einsum("crhab,cbp->hrap", mats, coeffs, preferred_element_type=f32)
    resid = both[0] - both[1] * energies
    grad = jnp.where(side == 0, resid / blocks, -(resid * energies) / blocks).astype(jnp.bfloat16)
    d_mats = jnp.einsum("rap,cbp->crab", grad, coeffs, preferred_element_type=f32)
    d_mats = d_mats.astype(jnp.bfloat16).reshape(blocks * blocks, a_count * orbitals)
    grad_second = jnp.dot(summed.T, d_mats, preferred_element_type=f32) / orbitals
    d_sum = lax.dot_general(d_mats, w_own, (((1,), (1,)), ((), ())), preferred_element_type=f32) / orbitals
    d_sum = d_sum.astype(jnp.bfloat16).reshape(n_dev, groups, hid)
    d_hidden = jnp.einsum("dgp,dgk->dpk", onehot, d_sum, preferred_element_type=f32).reshape(-1, hid)
    d_pre = (d_hidden * sig * (1.0 + pre * (1.0 - sig))).astype(jnp.bfloat16)
    term_first = jnp.dot(feats.T, d_pre, preferred_element_type=f32)
    mine = lax.dynamic_slice_in_dim(resid, side * (blocks // 2), blocks // 2, 0)
    mine = mine.reshape(half, blk_dev, a_count, columns)
    square = jnp.full((8, 128), 0.5 * jnp.sum(resid * resid), f32)
    first, loss_sum, residual = finish(n_dev, term_first.reshape(n_dev, width // n_dev, hid), square, mine)
    grad_first = first.reshape(width, hid)
    loss = loss_sum[0, :1] / (blocks * orbitals * columns)
    return (residual, loss, grad_first, grad_second)


def solution(mesh):
    in_specs = (
        P(("parts", "blk"), None),
        P(),
        P(),
        P(("parts", "blk"), None, None),
        P(),
        P(("parts", "blk"), None),
        P(("parts", "blk")),
        P(("parts", "blk")),
    )
    out_specs = (P(("parts", "blk"), None, None), P("parts"), P("parts", None), P("parts", "blk"))
    return jax.shard_map(
        fast_local if mesh.shape["blk"] == 16 else local, mesh=mesh, in_specs=in_specs, out_specs=out_specs, check_vma=False)
```

```python
import jax
import jax.numpy as jnp
from jax import lax
from jax.experimental import pallas as pl
from jax.experimental.pallas import tpu as pltpu
from jax.sharding import PartitionSpec as P


def predict(feats, w_first, w_second, orbitals):
    pre = jnp.dot(feats, w_first, preferred_element_type=jnp.float32)
    hidden = jax.nn.silu(pre).astype(jnp.bfloat16)
    blocks = (jnp.dot(hidden, w_second, preferred_element_type=jnp.float32) / orbitals).astype(
        jnp.bfloat16
    )
    return (pre, hidden, blocks)


def weight_terms(feats, pre, hidden, d_flat, w_second, orbitals):
    term_second = jnp.dot(hidden.T, d_flat, preferred_element_type=jnp.float32) / orbitals
    d_hidden = (
        lax.dot_general(
            d_flat, w_second, (((1,), (1,)), ((), ())), preferred_element_type=jnp.float32
        )
        / orbitals
    )
    sig = jax.nn.sigmoid(pre)
    d_pre = (d_hidden * sig * (1.0 + pre * (1.0 - sig))).astype(jnp.bfloat16)
    term_first = jnp.dot(feats.T, d_pre, preferred_element_type=jnp.float32)
    return (term_first, term_second)


def slot_work(slot_blocks, slot_panel, slot_rows, energies, blk_dev, total_blocks):
    slots, unused_two, orbitals, unused_o = slot_blocks.shape
    columns = slot_panel.shape[2]
    group = 32
    steps_count = slots // group
    grouped = (
        slot_blocks.reshape(steps_count, group, 2, orbitals, orbitals),
        slot_panel.reshape(steps_count, group, orbitals, columns),
        slot_rows.reshape(steps_count, group),
    )
    row_ids = jnp.arange(blk_dev, dtype=jnp.int32)

    def forward(total, item):
        blocks, coeffs, rows = item
        h_panel = jnp.einsum(
            "sab,sbp->sap", blocks[:, 0], coeffs, preferred_element_type=jnp.float32
        )
        s_panel = jnp.einsum(
            "sab,sbp->sap", blocks[:, 1], coeffs, preferred_element_type=jnp.float32
        )
        contrib = h_panel - s_panel * energies
        selector = (rows[None, :] == row_ids[:, None]).astype(jnp.float32)
        added = jnp.einsum("rs,sap->rap", selector, contrib, precision=lax.Precision.HIGHEST)
        return (total + added, None)

    residual = lax.scan(forward, jnp.zeros((blk_dev, orbitals, columns), jnp.float32), grouped)[0]
    grad_h = (residual / total_blocks).astype(jnp.bfloat16)
    grad_s = (-(residual * energies) / total_blocks).astype(jnp.bfloat16)

    def backward(carry, item):
        blocks, coeffs, rows = item
        valid = (rows >= 0)[:, None, None]
        safe_rows = jnp.maximum(rows, 0)
        gh_rows = jnp.where(valid, grad_h[safe_rows], jnp.zeros((), jnp.bfloat16))
        gs_rows = jnp.where(valid, grad_s[safe_rows], jnp.zeros((), jnp.bfloat16))
        d_h = jnp.einsum(
            "sap,sbp->sab", gh_rows, coeffs, preferred_element_type=jnp.float32
        ).astype(jnp.bfloat16)
        d_s = jnp.einsum(
            "sap,sbp->sab", gs_rows, coeffs, preferred_element_type=jnp.float32
        ).astype(jnp.bfloat16)
        return (carry, jnp.stack([d_h, d_s], axis=1))

    d_blocks = lax.scan(backward, 0, grouped)[1]
    return (residual, d_blocks.reshape(slots, 2, orbitals, orbitals))


def local(features, w_first, w_second, panel, energies, pair_dest, pair_row, pair_col):
    n_dev = lax.axis_size("blk")
    my_index = lax.axis_index("blk")
    pair_count, feat_width = features.shape
    blk_dev, orbitals, columns = panel.shape
    capacity = 3 * pair_count // (2 * n_dev)
    slots = n_dev * capacity
    total_blocks = blk_dev * n_dev
    dest = pair_dest[:, 0]
    dest_table = (dest[:, None] == jnp.arange(n_dev, dtype=jnp.int32)[None, :]).astype(jnp.int32)
    rank_in = jnp.sum(jnp.cumsum(dest_table, axis=0) * dest_table, axis=1) - 1
    slot_of = dest * capacity + rank_in
    source = (
        jnp.full((slots,), pair_count, jnp.int32)
        .at[slot_of]
        .set(jnp.arange(pair_count, dtype=jnp.int32))
    )
    empty_label = jnp.full((1,), -1, jnp.int32)
    rows_sent = jnp.concatenate([pair_row, empty_label])[source]
    cols_sent = jnp.concatenate([my_index * blk_dev + pair_col, jnp.zeros((1,), jnp.int32)])[source]
    labels = jnp.stack([rows_sent, cols_sent], axis=-1).reshape(n_dev, capacity, 2)
    whole_panel = lax.all_gather(panel, "blk", axis=0, tiled=True)
    pre, hidden, blocks = predict(features, w_first, w_second, orbitals)
    padded = jnp.concatenate([blocks, jnp.zeros((1, blocks.shape[1]), jnp.bfloat16)], axis=0)
    send_blocks = padded[source].reshape(n_dev, capacity, 2, orbitals, orbitals)
    got_blocks, got_labels = (
        lax.all_to_all(send_blocks, "blk", split_axis=0, concat_axis=0, tiled=True),
        lax.all_to_all(labels, "blk", split_axis=0, concat_axis=0, tiled=True),
    )
    got_labels = got_labels.reshape(slots, 2)
    slot_panel = whole_panel[got_labels[:, 1]]
    residual, d_blocks = slot_work(
        got_blocks.reshape(slots, 2, orbitals, orbitals),
        slot_panel,
        got_labels[:, 0],
        energies,
        blk_dev,
        total_blocks,
    )
    back = lax.all_to_all(
        d_blocks.reshape(n_dev, capacity, 2, orbitals, orbitals),
        "blk",
        split_axis=0,
        concat_axis=0,
        tiled=True,
    )
    d_flat = back.reshape(slots, 2 * orbitals * orbitals)[slot_of]
    term_first, term_second = weight_terms(features, pre, hidden, d_flat, w_second, orbitals)
    grad_second = lax.psum_scatter(term_second, "blk", scatter_dimension=1, tiled=True)
    grad_first, square_sum = lax.psum((term_first, jnp.sum(residual * residual)), "blk")
    loss = (square_sum / (total_blocks * orbitals * columns)).reshape(1)
    return (residual, loss, grad_first, grad_second)


VMEM = pl.BlockSpec(memory_space=pltpu.VMEM)
MESH = pl.DeviceIdType.MESH


def greet(partners):
    barrier = pltpu.get_barrier_semaphore()
    for other in partners:
        pl.semaphore_signal(barrier, inc=1, device_id={"blk": other}, device_id_type=MESH)
    pl.semaphore_wait(barrier, len(partners))


def gather_kernel(n, count, *refs):
    ins, outs = refs[:count], refs[count : 2 * count]
    send_sem, recv_sem, local_sem = refs[2 * count :]
    me = lax.axis_index("blk")
    depth = n // 4
    z, x, core = me // 4, (me // 2) % 2, me % 2

    def at(zz, xx, cc):
        return zz * 4 + xx * 2 + cc

    x_peer, core_peer = at(z, 1 - x, core), at(z, x, 1 - core)
    greet([x_peer, core_peer] + [at((z + d) % depth, x, core) for d in range(1, depth)])

    def copy(arr, source, block, peer, kind):
        return pltpu.make_async_remote_copy(
            src_ref=source,
            dst_ref=outs[arr].at[block],
            send_sem=send_sem.at[arr, block, kind],
            recv_sem=recv_sem.at[arr, block],
            device_id={"blk": peer},
            device_id_type=MESH,
        )

    def arrived(arr, block):
        copy(arr, outs[arr].at[block], block, core_peer, 0).wait_recv()

    def spread(arr, zz, act, up, down, source=None):
        block = at(zz, x, core)
        source = outs[arr].at[block] if source is None else source

        if up:

            @pl.when(z < depth - 1)
            def go_up():
                act(copy(arr, source, block, at(z + 1, x, core), 2))

        if down:

            @pl.when(z > 0)
            def go_down():
                act(copy(arr, source, block, at(z - 1, x, core), 3))

        act(copy(arr, source, block, x_peer, 0))
        act(copy(arr, source, block, core_peer, 1))

    def each_dist(fn):
        for dist in range(1, depth):

            @pl.when(z >= dist)
            def below(dist=dist):
                fn(z - dist, True, False)

            @pl.when(z + dist < depth)
            def above(dist=dist):
                fn(z + dist, False, True)

    begin = lambda item: item.start()
    ended = lambda item: item.wait_send()
    own = []
    for arr in range(count):
        spread(arr, z, begin, True, True, ins[arr])
        item = pltpu.make_async_copy(ins[arr], outs[arr].at[me], local_sem.at[arr])
        item.start()
        own.append(item)

    for arr in range(count):

        def relay(zz, up, down):
            arrived(arr, at(zz, x, core))
            spread(arr, zz, begin, up, down)

        each_dist(relay)

        def across(zz, up=False, down=False):
            block = at(zz, 1 - x, core)
            arrived(arr, block)
            begin(copy(arr, outs[arr].at[block], block, core_peer, 1))

        across(z)
        each_dist(across)
    for arr in range(count):
        for zz in range(depth):
            for xx in range(2):
                arrived(arr, at(zz, xx, 1 - core))
        own[arr].wait()
        spread(arr, z, ended, True, True, ins[arr])
        each_dist(lambda zz, up, down: spread(arr, zz, ended, up, down))
        for zz in range(depth):
            block = at(zz, 1 - x, core)
            ended(copy(arr, outs[arr].at[block], block, core_peer, 1))


def gather_all(n, arrays):
    count = len(arrays)
    return pl.pallas_call(
        lambda *refs: gather_kernel(n, count, *refs),
        out_shape=[jax.ShapeDtypeStruct((n,) + a.shape, a.dtype) for a in arrays],
        in_specs=[VMEM] * count,
        out_specs=[VMEM] * count,
        scratch_shapes=[
            pltpu.SemaphoreType.DMA((count, n, 4)),
            pltpu.SemaphoreType.DMA((count, n)),
            pltpu.SemaphoreType.DMA((count,)),
        ],
        compiler_params=pltpu.CompilerParams(
            collective_id=0, has_side_effects=True, vmem_limit_bytes=32 * 2**20
        ),
        name="gather_all",
    )(*arrays)


def finish_kernel(n, term, square, mine, first, loss, resid, land, loss_land, total, *sems):
    send_t, recv_t, send_l, recv_l, send_r, recv_r, send_g, recv_g = sems
    me = lax.axis_index("blk")
    half = n // 2
    side, spot = me // half, me % half
    rows = mine.shape[2]
    others = [(me + k) % n for k in range(1, n)]
    greet(others)

    def copy(src, dst, send_sem, recv_sem, peer):
        return pltpu.make_async_remote_copy(
            src_ref=src,
            dst_ref=dst,
            send_sem=send_sem,
            recv_sem=recv_sem,
            device_id={"blk": peer},
            device_id_type=MESH,
        )

    started = []
    for k, peer in enumerate(others):
        started.append(copy(term.at[peer], land.at[me], send_t.at[k], recv_t.at[me], peer))
        started.append(copy(square, loss_land.at[me], send_l.at[k], recv_l.at[me], peer))
    for k in range(1, half):
        near = (spot + k) % half
        started.append(
            copy(
                mine.at[near],
                resid.at[:, pl.ds(pl.multiple_of(spot * rows, 8), rows), :],
                send_r.at[k],
                recv_r.at[spot],
                side * half + near,
            )
        )
    for item in started:
        item.start()
    land[me] = term[me]
    loss_land[me] = square[...]
    resid[:, pl.ds(pl.multiple_of(spot * rows, 8), rows), :] = mine[spot]
    for peer in others:
        copy(term.at[me], land.at[peer], send_t.at[0], recv_t.at[peer], peer).wait_recv()
    added = land[0]
    for d in range(1, n):
        added = added + land[d]
    total[...] = added
    final = []
    for k, peer in enumerate(others):
        item = copy(total, first.at[me], send_g.at[k], recv_g.at[me], peer)
        item.start()
        final.append(item)
    first[me] = added
    for peer in others:
        copy(square, loss_land.at[peer], send_l.at[0], recv_l.at[peer], peer).wait_recv()
    squares = loss_land[0]
    for d in range(1, n):
        squares = squares + loss_land[d]
    loss[...] = squares
    for k in range(1, half):
        near = (spot + k) % half
        copy(
            mine.at[near],
            resid.at[:, pl.ds(pl.multiple_of(near * rows, 8), rows), :],
            send_r.at[k],
            recv_r.at[near],
            side * half + near,
        ).wait_recv()
    for peer in others:
        copy(total, first.at[peer], send_g.at[0], recv_g.at[peer], peer).wait_recv()
    for item in started + final:
        item.wait_send()


def finish(n, term, square, mine):
    half, blk_dev, rows, columns = mine.shape
    dma = pltpu.SemaphoreType.DMA
    return pl.pallas_call(
        lambda *refs: finish_kernel(n, *refs),
        out_shape=[
            jax.ShapeDtypeStruct(term.shape, jnp.float32),
            jax.ShapeDtypeStruct(square.shape, jnp.float32),
            jax.ShapeDtypeStruct((blk_dev, half * rows, columns), jnp.float32),
        ],
        in_specs=[VMEM] * 3,
        out_specs=[VMEM] * 3,
        scratch_shapes=[
            pltpu.VMEM(term.shape, jnp.float32),
            pltpu.VMEM((n,) + square.shape, jnp.float32),
            pltpu.VMEM(term.shape[1:], jnp.float32),
        ]
        + [dma((n,))] * 8,
        compiler_params=pltpu.CompilerParams(
            collective_id=1, has_side_effects=True, vmem_limit_bytes=32 * 2**20
        ),
        name="finish",
    )(term, square, mine)


def swap_halves(top, bottom):
    low = lax.broadcasted_iota(jnp.int32, top.shape, 1) < 64
    return (
        jnp.where(low, top, pltpu.roll(bottom, 64, 1)),
        jnp.where(low, pltpu.roll(top, 64, 1), bottom),
    )


def compute_kernel(
    n, blocks, a_count, feats, ids, coeffs, w_first, w_part, w_own, energies, grad_scale,
    second_out, first_out, resid_out, square_out, slope, summed, mats, d_mats, d_sum
):
    f32, bf16 = jnp.float32, jnp.bfloat16
    orbitals = 64
    groups = 2 * blocks
    lanes = 2 * orbitals
    pairs = feats.shape[1]

    def onehot(b):
        rows = lax.broadcasted_iota(jnp.int32, (groups, pairs), 0)
        return jnp.where(rows == ids[b][0:1, :], 1.0, 0.0).astype(bf16)

    def predict_block(b, carry):
        pre = jnp.dot(feats[b], w_first[...], preferred_element_type=f32)
        sig = 1.0 / (1.0 + jnp.exp(-pre))
        slope[b] = sig * (1.0 + pre * (1.0 - sig))
        hidden = (pre * sig).astype(bf16)
        total = jnp.dot(onehot(b), hidden, preferred_element_type=f32).astype(bf16)
        summed[pl.ds(pl.multiple_of(b * groups, groups), groups), :] = total
        made = jnp.dot(total, w_part[...], preferred_element_type=f32) / orbitals
        where_b = pl.ds(pl.multiple_of(b * lanes, lanes), lanes)
        for pair in range(a_count):
            slab = made[:, pair * lanes : (pair + 1) * lanes]
            even, odd = swap_halves(slab[:blocks], slab[blocks:])
            start = 2 * pair * blocks
            mats[start : start + blocks, where_b] = even.astype(bf16)
            mats[start + blocks : start + 2 * blocks, where_b] = odd.astype(bf16)
        return carry

    lax.fori_loop(0, n, predict_block, 0)
    rows = a_count * blocks
    h_part = jnp.dot(mats[:rows, :], coeffs[...], preferred_element_type=f32)
    s_part = jnp.dot(mats[rows:, :], coeffs[...], preferred_element_type=f32)
    resid = h_part - s_part * energies[...]
    resid_out[...] = resid
    square_out[...] = jnp.full(square_out.shape, 0.5 * jnp.sum(resid * resid), f32)
    grad = (resid * grad_scale[...]).astype(bf16)

    def back_block(b, carry):
        where_b = pl.ds(pl.multiple_of(b * lanes, lanes), lanes)
        got = lax.dot_general(
            grad, coeffs[where_b, :], (((1,), (1,)), ((), ())), preferred_element_type=f32
        )
        for pair in range(a_count // 2):
            start = 2 * pair * blocks
            even, odd = swap_halves(
                got[start : start + blocks], got[start + blocks : start + 2 * blocks]
            )
            cols = slice(pair * lanes, (pair + 1) * lanes)
            base = pl.multiple_of(b * groups, groups)
            d_mats[pl.ds(base, groups), cols] = jnp.concatenate([even, odd], axis=0).astype(bf16)
        return carry

    lax.fori_loop(0, n, back_block, 0)
    second_out[...] = (
        lax.dot_general(
            summed[...], d_mats[...], (((0,), (0,)), ((), ())), preferred_element_type=f32
        )
        / orbitals
    )
    d_sum[...] = (
        lax.dot_general(
            d_mats[...], w_own[...], (((1,), (1,)), ((), ())), preferred_element_type=f32
        )
        / orbitals
    ).astype(bf16)
    first_out[...] = jnp.zeros(first_out.shape, f32)

    def first_block(b, carry):
        part = d_sum[pl.ds(pl.multiple_of(b * groups, groups), groups), :]
        spread = lax.dot_general(
            onehot(b), part, (((0,), (0,)), ((), ())), preferred_element_type=f32
        )
        d_pre = (spread * slope[b]).astype(bf16)
        first_out[...] += lax.dot_general(
            feats[b], d_pre, (((0,), (0,)), ((), ())), preferred_element_type=f32
        )
        return carry

    lax.fori_loop(0, n, first_block, 0)


def compute(n, blocks, a_count, *args):
    feats, ids, coeffs, w_first, w_part, w_own = args[:6]
    f32, bf16 = jnp.float32, jnp.bfloat16
    width, hid = w_first.shape
    pairs = feats.shape[1]
    columns = coeffs.shape[1]
    shape = jax.ShapeDtypeStruct
    return pl.pallas_call(
        lambda *refs: compute_kernel(n, blocks, a_count, *refs),
        out_shape=[
            shape((hid, w_own.shape[1]), f32),
            shape((width, hid), f32),
            shape((a_count * blocks, columns), f32),
            shape((8, 128), f32),
        ],
        in_specs=[VMEM] * 8,
        out_specs=[VMEM] * 4,
        scratch_shapes=[
            pltpu.VMEM((n, pairs, hid), f32),
            pltpu.VMEM((blocks * blocks, hid), bf16),
            pltpu.VMEM((2 * a_count * blocks, coeffs.shape[0]), bf16),
            pltpu.VMEM((blocks * blocks, w_own.shape[1]), bf16),
            pltpu.VMEM((blocks * blocks, hid), bf16),
        ],
        compiler_params=pltpu.CompilerParams(vmem_limit_bytes=48 * 2**20),
        name="compute",
    )(*args)


def fast_local(features, w_first, w_second, panel, energies, pair_dest, pair_row, pair_col):
    n_dev = lax.axis_size("blk")
    me = lax.axis_index("blk")
    pairs, width = features.shape
    blk_dev, orbitals, columns = panel.shape
    hid = w_second.shape[0]
    blocks = blk_dev * n_dev
    half = n_dev // 2
    a_count = orbitals // half
    side = me // half
    spot = me % half
    f32 = jnp.float32
    gid = pair_col * blocks + pair_dest[:, 0] * blk_dev + pair_row
    ids = jnp.broadcast_to(gid.reshape(1, pairs), (8, pairs))
    feats, gids, coeffs = gather_all(
        n_dev, (features, ids, panel.reshape(blk_dev * orbitals, columns))
    )
    span = a_count * orbitals
    w_part = jnp.concatenate(
        [
            lax.dynamic_slice_in_dim(w_second, part * orbitals * orbitals + spot * span, span, 1)
            for part in range(2)
        ],
        axis=1,
    )
    w_own = lax.dynamic_slice_in_dim(w_second, me * span, span, 1)
    grad_scale = jnp.where(side == 0, jnp.ones_like(energies), -energies) / blocks
    grad_second, term_first, resid, square = compute(
        n_dev,
        blocks,
        a_count,
        feats,
        gids,
        coeffs.reshape(blocks * orbitals, columns),
        w_first,
        w_part,
        w_own,
        energies[None, :],
        grad_scale[None, :],
    )
    resid = resid.reshape(a_count, blocks, columns)
    mine = lax.dynamic_slice_in_dim(resid, side * (blocks // 2), blocks // 2, 1)
    mine = mine.transpose(1, 0, 2).reshape(half, blk_dev, a_count, columns)
    first, loss_sum, residual = finish(n_dev, term_first.reshape(n_dev, width // n_dev, hid), square, mine)
    grad_first = first.reshape(width, hid)
    loss = loss_sum[0, :1] / (blocks * orbitals * columns)
    return (residual, loss, grad_first, grad_second)


def solution(mesh):
    in_specs = (
        P(("parts", "blk"), None),
        P(),
        P(),
        P(("parts", "blk"), None, None),
        P(),
        P(("parts", "blk"), None),
        P(("parts", "blk")),
        P(("parts", "blk")),
    )
    out_specs = (P(("parts", "blk"), None, None), P("parts"), P("parts", None), P("parts", "blk"))
    return jax.shard_map(
        fast_local if mesh.shape["blk"] == 16 else local, mesh=mesh, in_specs=in_specs, out_specs=out_specs, check_vma=False)
```

```python
import jax
import jax.numpy as jnp
from jax import lax
from jax.experimental import pallas as pl
from jax.experimental.pallas import tpu as pltpu
from jax.sharding import PartitionSpec as P


def predict(feats, w_first, w_second, orbitals):
    pre = jnp.dot(feats, w_first, preferred_element_type=jnp.float32)
    hidden = jax.nn.silu(pre).astype(jnp.bfloat16)
    blocks = (jnp.dot(hidden, w_second, preferred_element_type=jnp.float32) / orbitals).astype(
        jnp.bfloat16
    )
    return (pre, hidden, blocks)


def weight_terms(feats, pre, hidden, d_flat, w_second, orbitals):
    term_second = jnp.dot(hidden.T, d_flat, preferred_element_type=jnp.float32) / orbitals
    d_hidden = (
        lax.dot_general(
            d_flat, w_second, (((1,), (1,)), ((), ())), preferred_element_type=jnp.float32
        )
        / orbitals
    )
    sig = jax.nn.sigmoid(pre)
    d_pre = (d_hidden * sig * (1.0 + pre * (1.0 - sig))).astype(jnp.bfloat16)
    term_first = jnp.dot(feats.T, d_pre, preferred_element_type=jnp.float32)
    return (term_first, term_second)


def slot_work(slot_blocks, slot_panel, slot_rows, energies, blk_dev, total_blocks):
    slots, unused_two, orbitals, unused_o = slot_blocks.shape
    columns = slot_panel.shape[2]
    group = 32
    steps_count = slots // group
    grouped = (
        slot_blocks.reshape(steps_count, group, 2, orbitals, orbitals),
        slot_panel.reshape(steps_count, group, orbitals, columns),
        slot_rows.reshape(steps_count, group),
    )
    row_ids = jnp.arange(blk_dev, dtype=jnp.int32)

    def forward(total, item):
        blocks, coeffs, rows = item
        h_panel = jnp.einsum(
            "sab,sbp->sap", blocks[:, 0], coeffs, preferred_element_type=jnp.float32
        )
        s_panel = jnp.einsum(
            "sab,sbp->sap", blocks[:, 1], coeffs, preferred_element_type=jnp.float32
        )
        contrib = h_panel - s_panel * energies
        selector = (rows[None, :] == row_ids[:, None]).astype(jnp.float32)
        added = jnp.einsum("rs,sap->rap", selector, contrib, precision=lax.Precision.HIGHEST)
        return (total + added, None)

    residual = lax.scan(forward, jnp.zeros((blk_dev, orbitals, columns), jnp.float32), grouped)[0]
    grad_h = (residual / total_blocks).astype(jnp.bfloat16)
    grad_s = (-(residual * energies) / total_blocks).astype(jnp.bfloat16)

    def backward(carry, item):
        blocks, coeffs, rows = item
        valid = (rows >= 0)[:, None, None]
        safe_rows = jnp.maximum(rows, 0)
        gh_rows = jnp.where(valid, grad_h[safe_rows], jnp.zeros((), jnp.bfloat16))
        gs_rows = jnp.where(valid, grad_s[safe_rows], jnp.zeros((), jnp.bfloat16))
        d_h = jnp.einsum(
            "sap,sbp->sab", gh_rows, coeffs, preferred_element_type=jnp.float32
        ).astype(jnp.bfloat16)
        d_s = jnp.einsum(
            "sap,sbp->sab", gs_rows, coeffs, preferred_element_type=jnp.float32
        ).astype(jnp.bfloat16)
        return (carry, jnp.stack([d_h, d_s], axis=1))

    d_blocks = lax.scan(backward, 0, grouped)[1]
    return (residual, d_blocks.reshape(slots, 2, orbitals, orbitals))


def local(features, w_first, w_second, panel, energies, pair_dest, pair_row, pair_col):
    n_dev = lax.axis_size("blk")
    my_index = lax.axis_index("blk")
    pair_count, feat_width = features.shape
    blk_dev, orbitals, columns = panel.shape
    capacity = 3 * pair_count // (2 * n_dev)
    slots = n_dev * capacity
    total_blocks = blk_dev * n_dev
    dest = pair_dest[:, 0]
    dest_table = (dest[:, None] == jnp.arange(n_dev, dtype=jnp.int32)[None, :]).astype(jnp.int32)
    rank_in = jnp.sum(jnp.cumsum(dest_table, axis=0) * dest_table, axis=1) - 1
    slot_of = dest * capacity + rank_in
    source = (
        jnp.full((slots,), pair_count, jnp.int32)
        .at[slot_of]
        .set(jnp.arange(pair_count, dtype=jnp.int32))
    )
    empty_label = jnp.full((1,), -1, jnp.int32)
    rows_sent = jnp.concatenate([pair_row, empty_label])[source]
    cols_sent = jnp.concatenate([my_index * blk_dev + pair_col, jnp.zeros((1,), jnp.int32)])[source]
    labels = jnp.stack([rows_sent, cols_sent], axis=-1).reshape(n_dev, capacity, 2)
    whole_panel = lax.all_gather(panel, "blk", axis=0, tiled=True)
    pre, hidden, blocks = predict(features, w_first, w_second, orbitals)
    padded = jnp.concatenate([blocks, jnp.zeros((1, blocks.shape[1]), jnp.bfloat16)], axis=0)
    send_blocks = padded[source].reshape(n_dev, capacity, 2, orbitals, orbitals)
    got_blocks, got_labels = (
        lax.all_to_all(send_blocks, "blk", split_axis=0, concat_axis=0, tiled=True),
        lax.all_to_all(labels, "blk", split_axis=0, concat_axis=0, tiled=True),
    )
    got_labels = got_labels.reshape(slots, 2)
    slot_panel = whole_panel[got_labels[:, 1]]
    residual, d_blocks = slot_work(
        got_blocks.reshape(slots, 2, orbitals, orbitals),
        slot_panel,
        got_labels[:, 0],
        energies,
        blk_dev,
        total_blocks,
    )
    back = lax.all_to_all(
        d_blocks.reshape(n_dev, capacity, 2, orbitals, orbitals),
        "blk",
        split_axis=0,
        concat_axis=0,
        tiled=True,
    )
    d_flat = back.reshape(slots, 2 * orbitals * orbitals)[slot_of]
    term_first, term_second = weight_terms(features, pre, hidden, d_flat, w_second, orbitals)
    grad_second = lax.psum_scatter(term_second, "blk", scatter_dimension=1, tiled=True)
    grad_first, square_sum = lax.psum((term_first, jnp.sum(residual * residual)), "blk")
    loss = (square_sum / (total_blocks * orbitals * columns)).reshape(1)
    return (residual, loss, grad_first, grad_second)


VMEM = pl.BlockSpec(memory_space=pltpu.VMEM)
MESH = pl.DeviceIdType.MESH


def greet(partners):
    barrier = pltpu.get_barrier_semaphore()
    for other in partners:
        pl.semaphore_signal(barrier, inc=1, device_id={"blk": other}, device_id_type=MESH)
    pl.semaphore_wait(barrier, len(partners))


def gather_kernel(n, count, *refs):
    ins, outs = refs[:count], refs[count : 2 * count]
    send_sem, recv_sem, local_sem = refs[2 * count :]
    me = lax.axis_index("blk")
    depth = n // 4
    z, x, core = me // 4, (me // 2) % 2, me % 2

    def at(zz, xx, cc):
        return zz * 4 + xx * 2 + cc

    x_peer, core_peer = at(z, 1 - x, core), at(z, x, 1 - core)
    low, high = z % 2, z // 2
    others = [(1 - low) + 2 * high, low + 2 * (1 - high), (1 - low) + 2 * (1 - high)]
    z_peers = [at(zz, x, core) for zz in others]
    greet([x_peer, core_peer] + z_peers)

    def copy(arr, source, block, peer, kind):
        return pltpu.make_async_remote_copy(
            src_ref=source,
            dst_ref=outs[arr].at[block],
            send_sem=send_sem.at[arr, block, kind],
            recv_sem=recv_sem.at[arr, block],
            device_id={"blk": peer},
            device_id_type=MESH,
        )

    started = []

    def send(arr, block, peer, kind, source=None):
        item = copy(arr, outs[arr].at[block] if source is None else source, block, peer, kind)
        item.start()
        started.append(item)

    def arrived(arr, block):
        copy(arr, outs[arr].at[block], block, core_peer, 0).wait_recv()

    own = []
    for arr in range(count):
        for k, peer in enumerate(z_peers):
            send(arr, me, peer, 2 + k, ins[arr])
        send(arr, me, x_peer, 0, ins[arr])
        send(arr, me, core_peer, 1, ins[arr])
        item = pltpu.make_async_copy(ins[arr], outs[arr].at[me], local_sem.at[arr])
        item.start()
        own.append(item)
    for arr in range(count):
        arrived(arr, x_peer)
        send(arr, x_peer, core_peer, 1)
        for block in z_peers:
            arrived(arr, block)
            send(arr, block, x_peer, 0)
            send(arr, block, core_peer, 1)
    for arr in range(count):
        for zz in others:
            block = at(zz, 1 - x, core)
            arrived(arr, block)
            send(arr, block, core_peer, 1)
    for arr in range(count):
        for d in range(depth):
            for xx in range(2):
                arrived(arr, at((z + d) % depth, xx, 1 - core))
        own[arr].wait()
    for item in started:
        item.wait_send()


def gather_all(n, arrays):
    count = len(arrays)
    return pl.pallas_call(
        lambda *refs: gather_kernel(n, count, *refs),
        out_shape=[jax.ShapeDtypeStruct((n,) + a.shape, a.dtype) for a in arrays],
        in_specs=[VMEM] * count,
        out_specs=[VMEM] * count,
        scratch_shapes=[
            pltpu.SemaphoreType.DMA((count, n, 1 + n // 4)),
            pltpu.SemaphoreType.DMA((count, n)),
            pltpu.SemaphoreType.DMA((count,)),
        ],
        compiler_params=pltpu.CompilerParams(
            collective_id=0, has_side_effects=True, vmem_limit_bytes=32 * 2**20
        ),
        name="gather_all",
    )(*arrays)


def finish_kernel(n, term, square, mine, first, loss, resid, land, loss_land, total, *sems):
    send_t, recv_t, send_l, recv_l, send_r, recv_r, send_g, recv_g = sems
    me = lax.axis_index("blk")
    half = n // 2
    side, spot = me // half, me % half
    rows = mine.shape[2]
    others = [(me + k) % n for k in range(1, n)]
    greet(others)

    def copy(src, dst, send_sem, recv_sem, peer):
        return pltpu.make_async_remote_copy(
            src_ref=src,
            dst_ref=dst,
            send_sem=send_sem,
            recv_sem=recv_sem,
            device_id={"blk": peer},
            device_id_type=MESH,
        )

    started = []
    for k, peer in enumerate(others):
        started.append(copy(term.at[peer], land.at[me], send_t.at[k], recv_t.at[me], peer))
        started.append(copy(square, loss_land.at[me], send_l.at[k], recv_l.at[me], peer))
    for k in range(1, half):
        near = (spot + k) % half
        started.append(
            copy(
                mine.at[near],
                resid.at[:, pl.ds(pl.multiple_of(spot * rows, 8), rows), :],
                send_r.at[k],
                recv_r.at[spot],
                side * half + near,
            )
        )
    for item in started:
        item.start()
    land[me] = term[me]
    loss_land[me] = square[...]
    resid[:, pl.ds(pl.multiple_of(spot * rows, 8), rows), :] = mine[spot]
    for peer in others:
        copy(term.at[me], land.at[peer], send_t.at[0], recv_t.at[peer], peer).wait_recv()
    added = land[0]
    for d in range(1, n):
        added = added + land[d]
    total[...] = added
    final = []
    for k, peer in enumerate(others):
        item = copy(total, first.at[me], send_g.at[k], recv_g.at[me], peer)
        item.start()
        final.append(item)
    first[me] = added
    for peer in others:
        copy(square, loss_land.at[peer], send_l.at[0], recv_l.at[peer], peer).wait_recv()
    squares = loss_land[0]
    for d in range(1, n):
        squares = squares + loss_land[d]
    loss[...] = squares
    for k in range(1, half):
        near = (spot + k) % half
        copy(
            mine.at[near],
            resid.at[:, pl.ds(pl.multiple_of(near * rows, 8), rows), :],
            send_r.at[k],
            recv_r.at[near],
            side * half + near,
        ).wait_recv()
    for peer in others:
        copy(total, first.at[peer], send_g.at[0], recv_g.at[peer], peer).wait_recv()
    for item in started + final:
        item.wait_send()


def finish(n, term, square, mine):
    half, blk_dev, rows, columns = mine.shape
    dma = pltpu.SemaphoreType.DMA
    return pl.pallas_call(
        lambda *refs: finish_kernel(n, *refs),
        out_shape=[
            jax.ShapeDtypeStruct(term.shape, jnp.float32),
            jax.ShapeDtypeStruct(square.shape, jnp.float32),
            jax.ShapeDtypeStruct((blk_dev, half * rows, columns), jnp.float32),
        ],
        in_specs=[VMEM] * 3,
        out_specs=[VMEM] * 3,
        scratch_shapes=[
            pltpu.VMEM(term.shape, jnp.float32),
            pltpu.VMEM((n,) + square.shape, jnp.float32),
            pltpu.VMEM(term.shape[1:], jnp.float32),
        ]
        + [dma((n,))] * 8,
        compiler_params=pltpu.CompilerParams(
            collective_id=1, has_side_effects=True, vmem_limit_bytes=32 * 2**20
        ),
        name="finish",
    )(term, square, mine)


def swap_halves(top, bottom):
    low = lax.broadcasted_iota(jnp.int32, top.shape, 1) < 64
    return (
        jnp.where(low, top, pltpu.roll(bottom, 64, 1)),
        jnp.where(low, pltpu.roll(top, 64, 1), bottom),
    )


def compute_kernel(
    n, blocks, a_count, feats, ids, coeffs, w_first, w_part, w_own, energies, grad_scale,
    second_out, first_out, resid_out, square_out, slope, summed, mats, d_mats, d_sum
):
    f32, bf16 = jnp.float32, jnp.bfloat16
    orbitals = 64
    groups = 2 * blocks
    lanes = 2 * orbitals
    pairs = feats.shape[1]

    def onehot(b):
        rows = lax.broadcasted_iota(jnp.int32, (groups, pairs), 0)
        return jnp.where(rows == ids[b][0:1, :], 1.0, 0.0).astype(bf16)

    def predict_block(b, carry):
        pre = jnp.dot(feats[b], w_first[...], preferred_element_type=f32)
        sig = 1.0 / (1.0 + jnp.exp(-pre))
        slope[b] = sig * (1.0 + pre * (1.0 - sig))
        hidden = (pre * sig).astype(bf16)
        total = jnp.dot(onehot(b), hidden, preferred_element_type=f32).astype(bf16)
        summed[pl.ds(pl.multiple_of(b * groups, groups), groups), :] = total
        made = jnp.dot(total, w_part[...], preferred_element_type=f32) / orbitals
        where_b = pl.ds(pl.multiple_of(b * lanes, lanes), lanes)
        for pair in range(a_count):
            slab = made[:, pair * lanes : (pair + 1) * lanes]
            even, odd = swap_halves(slab[:blocks], slab[blocks:])
            start = 2 * pair * blocks
            mats[start : start + blocks, where_b] = even.astype(bf16)
            mats[start + blocks : start + 2 * blocks, where_b] = odd.astype(bf16)
        return carry

    lax.fori_loop(0, n, predict_block, 0)
    rows = a_count * blocks
    h_part = jnp.dot(mats[:rows, :], coeffs[...], preferred_element_type=f32)
    s_part = jnp.dot(mats[rows:, :], coeffs[...], preferred_element_type=f32)
    resid = h_part - s_part * energies[...]
    resid_out[...] = resid
    square_out[...] = jnp.full(square_out.shape, 0.5 * jnp.sum(resid * resid), f32)
    grad = (resid * grad_scale[...]).astype(bf16)

    def back_block(b, carry):
        where_b = pl.ds(pl.multiple_of(b * lanes, lanes), lanes)
        got = lax.dot_general(
            grad, coeffs[where_b, :], (((1,), (1,)), ((), ())), preferred_element_type=f32
        )
        for pair in range(a_count // 2):
            start = 2 * pair * blocks
            even, odd = swap_halves(
                got[start : start + blocks], got[start + blocks : start + 2 * blocks]
            )
            cols = slice(pair * lanes, (pair + 1) * lanes)
            base = pl.multiple_of(b * groups, groups)
            d_mats[pl.ds(base, groups), cols] = jnp.concatenate([even, odd], axis=0).astype(bf16)
        return carry

    lax.fori_loop(0, n, back_block, 0)
    second_out[...] = (
        lax.dot_general(
            summed[...], d_mats[...], (((0,), (0,)), ((), ())), preferred_element_type=f32
        )
        / orbitals
    )
    d_sum[...] = (
        lax.dot_general(
            d_mats[...], w_own[...], (((1,), (1,)), ((), ())), preferred_element_type=f32
        )
        / orbitals
    ).astype(bf16)
    first_out[...] = jnp.zeros(first_out.shape, f32)

    def first_block(b, carry):
        part = d_sum[pl.ds(pl.multiple_of(b * groups, groups), groups), :]
        spread = lax.dot_general(
            onehot(b), part, (((0,), (0,)), ((), ())), preferred_element_type=f32
        )
        d_pre = (spread * slope[b]).astype(bf16)
        first_out[...] += lax.dot_general(
            feats[b], d_pre, (((0,), (0,)), ((), ())), preferred_element_type=f32
        )
        return carry

    lax.fori_loop(0, n, first_block, 0)


def compute(n, blocks, a_count, *args):
    feats, ids, coeffs, w_first, w_part, w_own = args[:6]
    f32, bf16 = jnp.float32, jnp.bfloat16
    width, hid = w_first.shape
    pairs = feats.shape[1]
    columns = coeffs.shape[1]
    shape = jax.ShapeDtypeStruct
    return pl.pallas_call(
        lambda *refs: compute_kernel(n, blocks, a_count, *refs),
        out_shape=[
            shape((hid, w_own.shape[1]), f32),
            shape((width, hid), f32),
            shape((a_count * blocks, columns), f32),
            shape((8, 128), f32),
        ],
        in_specs=[VMEM] * 8,
        out_specs=[VMEM] * 4,
        scratch_shapes=[
            pltpu.VMEM((n, pairs, hid), f32),
            pltpu.VMEM((blocks * blocks, hid), bf16),
            pltpu.VMEM((2 * a_count * blocks, coeffs.shape[0]), bf16),
            pltpu.VMEM((blocks * blocks, w_own.shape[1]), bf16),
            pltpu.VMEM((blocks * blocks, hid), bf16),
        ],
        compiler_params=pltpu.CompilerParams(vmem_limit_bytes=48 * 2**20),
        name="compute",
    )(*args)


def fast_local(features, w_first, w_second, panel, energies, pair_dest, pair_row, pair_col):
    n_dev = lax.axis_size("blk")
    me = lax.axis_index("blk")
    pairs, width = features.shape
    blk_dev, orbitals, columns = panel.shape
    hid = w_second.shape[0]
    blocks = blk_dev * n_dev
    half = n_dev // 2
    a_count = orbitals // half
    side = me // half
    spot = me % half
    f32 = jnp.float32
    gid = pair_col * blocks + pair_dest[:, 0] * blk_dev + pair_row
    ids = jnp.broadcast_to(gid.reshape(1, pairs), (8, pairs))
    feats, gids, coeffs = gather_all(
        n_dev, (features, ids, panel.reshape(blk_dev * orbitals, columns))
    )
    span = a_count * orbitals
    w_part = jnp.concatenate(
        [
            lax.dynamic_slice_in_dim(w_second, part * orbitals * orbitals + spot * span, span, 1)
            for part in range(2)
        ],
        axis=1,
    )
    w_own = lax.dynamic_slice_in_dim(w_second, me * span, span, 1)
    grad_scale = jnp.where(side == 0, jnp.ones_like(energies), -energies) / blocks
    grad_second, term_first, resid, square = compute(
        n_dev,
        blocks,
        a_count,
        feats,
        gids,
        coeffs.reshape(blocks * orbitals, columns),
        w_first,
        w_part,
        w_own,
        energies[None, :],
        grad_scale[None, :],
    )
    resid = resid.reshape(a_count, blocks, columns)
    mine = lax.dynamic_slice_in_dim(resid, side * (blocks // 2), blocks // 2, 1)
    mine = mine.transpose(1, 0, 2).reshape(half, blk_dev, a_count, columns)
    first, loss_sum, residual = finish(n_dev, term_first.reshape(n_dev, width // n_dev, hid), square, mine)
    grad_first = first.reshape(width, hid)
    loss = loss_sum[0, :1] / (blocks * orbitals * columns)
    return (residual, loss, grad_first, grad_second)


def solution(mesh):
    in_specs = (
        P(("parts", "blk"), None),
        P(),
        P(),
        P(("parts", "blk"), None, None),
        P(),
        P(("parts", "blk"), None),
        P(("parts", "blk")),
        P(("parts", "blk")),
    )
    out_specs = (P(("parts", "blk"), None, None), P("parts"), P("parts", None), P("parts", "blk"))
    return jax.shard_map(
        fast_local if mesh.shape["blk"] == 16 else local, mesh=mesh, in_specs=in_specs, out_specs=out_specs, check_vma=False)
```
